32 devices in a mesh: seq: 8 (over y, x, core), head: 4 (over z).
Axes of the slice: x: 2, y: 2, z: 4, core: 2. Of those that a mesh axis runs over, the one named last changes fastest.
Arguments:
- activations: bfloat16 [4096, 5376], P(('seq', 'head')), may hold values from -42 to 42, as said below
- input_gain: float32 [5376], replicated, may hold values from 0.1 to 1.9
- query_weight: bfloat16 [5376, 4096], P(None, 'head'), may hold values from -2.2818633 to 2.2818633
- key_weight: bfloat16 [5376, 2048], P(None, 'head'), may hold values from -1 to 1
- value_weight: bfloat16 [5376, 2048], P(None, 'head'), may hold values from -0.078125 to 0.078125
- output_weight: bfloat16 [4096, 5376], P('head'), may hold values from -0.09375 to 0.09375
- cache_edge: bfloat16 [2, 1024, 2048], P(None, None, 'head'), may hold values from -6 to 6
- post_gain: float32 [5376], replicated, may hold values from 0.1 to 1.9
Outputs:
- layer_out: bfloat16 [4096, 5376], P(('seq', 'head'))
The draws below stay inside these ranges and needn't reach their ends.
Inputs may be any that keep to these rules, and one draw needn't show every extreme that they name: `activations`: input rows with row and feature scales.
All inputs are finite; a program needn't handle non-finite values.
Results may differ from the reference program's by a relative error of at most 0.006.
Values may be sent and summed in bfloat16 or wider, within the bound.
A program may use at most 128 MiB of HBM per device.

```python
import math
import jax
import jax.numpy as jnp
from jax import lax

D = 5376
QH = 32
KVH = 16
HD = 128
WINDOW = 1024
SCALAR = 168
TOK_DEV = 512
TOKENS = 4096
N_SEQ = 8


def key_matrix(key):
    base = jnp.clip(jax.random.normal(jax.random.fold_in(key, 7), (D, KVH * HD), jnp.float32), -4.0, 4.0)
    return base * D ** (-0.5)


def draw_activations(key, part):
    first, second, third = jax.random.split(key, 3)
    row_scale = jnp.exp(jax.random.uniform(first, (TOKENS, 1), jnp.float32, math.log(0.32), math.log(3.2)))
    column_scale = jnp.exp(jax.random.uniform(second, (1, D), jnp.float32, math.log(0.32), math.log(3.2)))
    base = jnp.clip(jax.random.normal(third, (TOKENS, D), jnp.float32), -4.0, 4.0)
    return (base * row_scale * column_scale).astype(jnp.bfloat16)


def draw_key_weight(key, part):
    return key_matrix(key).astype(jnp.bfloat16)


def draw_query_weight(key, part):
    base = jnp.clip(jax.random.normal(jax.random.fold_in(key, 11), (D, QH * HD), jnp.float32), -4.0, 4.0) * D ** (-0.5)
    return base.astype(jnp.bfloat16)


def shard_levels(stream_key, shape, pieces, least, top_value):
    def one(position, blocks):
        heights = jax.random.uniform(jax.random.fold_in(jax.random.fold_in(stream_key, 6), position), (blocks,), jnp.float32, least / len(pieces), top_value / len(pieces))
        return jnp.repeat(jnp.exp(heights), shape[position] // blocks).reshape((-1,) + (1,) * (len(shape) - position - 1))

    level = one(*pieces[0])
    for cut in pieces[1:]:
        level = level * one(*cut)
    return level


def normal_values(key, extent, width, bound, cuts=(), kind=jnp.bfloat16):
    loudness = shard_levels(key, extent, cuts, -0.22, 0.18) if cuts else 1.0
    values = jax.random.normal(key, extent, jnp.float32) * width * loudness
    return jnp.minimum(jnp.maximum(values, -bound), bound).astype(kind)


def setup_inputs(seed: int = 0) -> dict:
    splits = jax.random.split(jax.random.key(seed), 9)
    return {
        "activations": draw_activations(jax.random.fold_in(splits[8], 71), 0),
        "input_gain": jnp.clip(1.0 + 0.18 * jax.random.normal(splits[1], (D,), jnp.float32), 0.1, 1.9),
        "query_weight": draw_query_weight(jax.random.fold_in(splits[8], 71), 0),
        "key_weight": draw_key_weight(jax.random.fold_in(splits[8], 71), 0),
        "value_weight": normal_values(splits[4], (D, KVH * HD), D ** -0.5, 0.078125, ((1, 4),)),
        "output_weight": normal_values(splits[5], (QH * HD, D), (QH * HD) ** -0.5, 0.09375, ((0, 4),)),
        "cache_edge": normal_values(splits[6], (2, WINDOW, KVH * HD), 1.0, 6.0, ((2, 4),)),
        "post_gain": jnp.clip(1.0 + 0.18 * jax.random.normal(splits[7], (D,), jnp.float32), 0.1, 1.9),
    }


EPSILON = 1e-06
ROPE_BASE = 10000.0

def normalize_rows(values, gain):
    return values * lax.rsqrt(lax.optimization_barrier(jnp.mean(values * values, axis=-1, keepdims=True)) + EPSILON) * gain

def rotate(vectors, positions):
    half_size = vectors.shape[-1] // 2
    frequency = ROPE_BASE ** (-(jnp.arange(half_size, dtype=jnp.float32) * 2.0 / vectors.shape[-1]))
    angles = positions[:, None] * frequency[None, :]
    cosine = jnp.cos(angles)[:, None, :]
    sine_part = jnp.sin(angles)[:, None, :]
    first_half = vectors[..., :half_size]
    second_half = vectors[..., half_size:]
    return jnp.concatenate([first_half * cosine - second_half * sine_part, second_half * cosine + first_half * sine_part], axis=-1)

def reference(activations, input_gain, query_weight, key_weight, value_weight, output_weight, cache_edge, post_gain):
    residual = activations.astype(jnp.float32)
    normed = normalize_rows(residual, input_gain).astype(jnp.bfloat16)
    queries_raw = jnp.dot(normed, query_weight, preferred_element_type=jnp.float32)
    keys_raw = jnp.dot(normed, key_weight, preferred_element_type=jnp.float32)
    value_rows = jnp.dot(normed, value_weight, preferred_element_type=jnp.float32)
    positions = jnp.arange(TOKENS, dtype=jnp.int32).astype(jnp.float32)
    queries = (rotate(queries_raw.reshape(TOKENS, QH, HD), positions) * SCALAR ** (-0.5)).astype(jnp.bfloat16)
    keys = rotate(keys_raw.reshape(TOKENS, KVH, HD), positions).astype(jnp.bfloat16)
    values = value_rows.astype(jnp.bfloat16).reshape(TOKENS, KVH, HD)
    all_keys = jnp.concatenate([cache_edge[0].reshape(WINDOW, KVH, HD), keys], axis=0)
    all_values = jnp.concatenate([cache_edge[1].reshape(WINDOW, KVH, HD), values], axis=0)
    group_size = QH // KVH
    query_index = jnp.arange(TOK_DEV, dtype=jnp.int32)
    key_index = jnp.arange(WINDOW + TOK_DEV, dtype=jnp.int32)
    allowed = (key_index[None, :] > query_index[:, None]) & (key_index[None, :] <= query_index[:, None] + WINDOW)

    def one_block(block_index):
        first_row = (block_index * TOK_DEV).astype(jnp.int32)
        query_block = lax.dynamic_slice_in_dim(queries, first_row, TOK_DEV, 0).reshape(TOK_DEV, KVH, group_size, HD)
        key_block = lax.dynamic_slice_in_dim(all_keys, first_row, WINDOW + TOK_DEV, 0)
        value_block = lax.dynamic_slice_in_dim(all_values, first_row, WINDOW + TOK_DEV, 0)
        scores = jnp.einsum('qgrd,kgd->grqk', query_block.astype(jnp.float32), key_block.astype(jnp.float32))
        scores = jnp.where(allowed[None, None], scores, -jnp.inf)
        largest = lax.optimization_barrier(jnp.max(scores, axis=-1, keepdims=True))
        exps = jnp.exp(scores - largest)
        probabilities = (exps / lax.optimization_barrier(jnp.sum(exps, axis=-1, keepdims=True))).astype(jnp.bfloat16)
        attended = jnp.einsum('grqk,kgd->qgrd', probabilities.astype(jnp.float32), value_block.astype(jnp.float32))
        return attended.astype(jnp.bfloat16).reshape(TOK_DEV, QH * HD)
    attended = lax.map(one_block, jnp.arange(N_SEQ, dtype=jnp.int32)).reshape(TOKENS, QH * HD)
    projected = jnp.dot(attended, output_weight, preferred_element_type=jnp.float32)
    branch = normalize_rows(projected, post_gain)
    return (residual + branch).astype(jnp.bfloat16)
```

```python
import jax
import jax.numpy as jnp
from jax import lax
from jax.sharding import PartitionSpec as P

HD = 128
WINDOW = 1024
SCALAR = 168
TOK_DEV = 512


EPSILON = 1e-06
ROPE_BASE = 10000.0


def from_behind(array, axis, by):
    count = lax.axis_size(axis)
    pairs = [(i, i + by) for i in range(count) if 0 <= i + by < count]
    return lax.ppermute(array, axis, pairs)


def normalize_rows(values, gain):
    return values * lax.rsqrt(jnp.mean(values * values, axis=-1, keepdims=True) + EPSILON) * gain


def rotate(vectors, positions):
    half_size = vectors.shape[-1] // 2
    frequency = ROPE_BASE ** (-(jnp.arange(half_size, dtype=jnp.float32) * 2.0 / vectors.shape[-1]))
    angles = positions[:, None] * frequency[None, :]
    cosine = jnp.cos(angles)[:, None, :]
    sine_part = jnp.sin(angles)[:, None, :]
    first_half = vectors[..., :half_size]
    second_half = vectors[..., half_size:]
    return jnp.concatenate(
        [
            first_half * cosine - second_half * sine_part,
            second_half * cosine + first_half * sine_part,
        ],
        axis=-1,
    )


def per_device(
    activations,
    input_gain,
    query_weight,
    key_weight,
    value_weight,
    output_weight,
    cache_edge,
    post_gain,
):
    heads_query = query_weight.shape[1] // HD
    heads_kv = key_weight.shape[1] // HD
    group_size = heads_query // heads_kv
    query_width = heads_query * HD
    kv_width = heads_kv * HD
    seq_pos = lax.axis_index("seq")
    first_pos = seq_pos * TOK_DEV
    normed = normalize_rows(activations.astype(jnp.float32), input_gain).astype(jnp.bfloat16)
    normed = lax.all_gather(normed, "head", axis=0, tiled=True)
    row_count = normed.shape[0]
    positions = (first_pos + jnp.arange(row_count, dtype=jnp.int32)).astype(jnp.float32)
    queries_raw = jnp.dot(normed, query_weight, preferred_element_type=jnp.float32)
    keys_raw = jnp.dot(normed, key_weight, preferred_element_type=jnp.float32)
    value_rows = jnp.dot(normed, value_weight, preferred_element_type=jnp.float32)
    queries = rotate(queries_raw.reshape(row_count, heads_query, HD), positions) * SCALAR ** (-0.5)
    keys = rotate(keys_raw.reshape(row_count, heads_kv, HD), positions)
    joined = jnp.concatenate(
        [queries.reshape(row_count, query_width), keys.reshape(row_count, kv_width), value_rows],
        axis=1,
    )
    packed = joined.astype(jnp.bfloat16)
    queries = packed[:, :query_width]
    own_edge = packed[:, query_width:]
    cache_rows = jnp.concatenate([cache_edge[0], cache_edge[1]], axis=1)
    reach_steps = WINDOW // TOK_DEV
    earlier = []
    received = own_edge
    for distance in range(1, reach_steps + 1):
        received = from_behind(own_edge, "seq", distance)
        offset = jnp.clip(WINDOW + (seq_pos - distance) * TOK_DEV, 0, WINDOW - TOK_DEV)
        from_cache = lax.dynamic_slice_in_dim(cache_rows, offset, TOK_DEV, 0)
        earlier.append(jnp.where(seq_pos >= distance, received, from_cache))
    window_rows = jnp.concatenate(earlier[::-1] + [own_edge], axis=0)
    span_length = window_rows.shape[0]
    key_rows = window_rows[:, :kv_width].reshape(span_length, heads_kv, HD)
    value_block = window_rows[:, kv_width:].reshape(span_length, heads_kv, HD)
    query_block = queries.reshape(TOK_DEV, heads_kv, group_size, HD)
    query_index = jnp.arange(TOK_DEV, dtype=jnp.int32)
    key_index = jnp.arange(span_length, dtype=jnp.int32)
    allowed = (key_index[None, :] > query_index[:, None]) & (
        key_index[None, :] <= query_index[:, None] + WINDOW
    )
    scores = jnp.einsum("qgrd,kgd->grqk", query_block, key_rows, preferred_element_type=jnp.float32)
    scores = jnp.where(allowed[None, None], scores, -jnp.inf)
    largest = jnp.max(scores, axis=-1, keepdims=True)
    exps = jnp.exp(scores - largest)
    probabilities = (exps / jnp.sum(exps, axis=-1, keepdims=True)).astype(jnp.bfloat16)
    attended = jnp.einsum(
        "grqk,kgd->qgrd", probabilities, value_block, preferred_element_type=jnp.float32
    )
    attended = attended.astype(jnp.bfloat16).reshape(TOK_DEV, query_width)
    projected = lax.psum_scatter(
        jnp.dot(attended, output_weight, preferred_element_type=jnp.float32).astype(jnp.bfloat16),
        "head",
        scatter_dimension=0,
        tiled=True,
    ).astype(jnp.float32)
    branch = normalize_rows(projected, post_gain)
    return (activations.astype(jnp.float32) + branch).astype(jnp.bfloat16)


def solution(mesh):
    return jax.shard_map(
        per_device,
        mesh=mesh,
        in_specs=(
            P(("seq", "head"), None),
            P(),
            P(None, "head"),
            P(None, "head"),
            P(None, "head"),
            P("head", None),
            P(None, None, "head"),
            P(),
        ),
        out_specs=P(("seq", "head"), None),
        check_vma=False,
    )
```

```python
import functools
import jax
import jax.numpy as jnp
from jax import lax
from jax.experimental import pallas as pl
from jax.experimental.pallas import tpu as pltpu
from jax.sharding import PartitionSpec as P

HD = 128
WINDOW = 1024
SCALAR = 168
TOK_DEV = 512
EPSILON = 1e-06
ROPE_BASE = 10000.0
REACH = WINDOW // TOK_DEV
ROW_CHUNKS = 2
COL_CHUNKS = 3
MESH = pl.DeviceIdType.MESH


def rope_tables(positions):
    half_size = HD // 2
    frequency = ROPE_BASE ** (-(jnp.arange(half_size, dtype=jnp.float32) * 2.0 / HD))
    angles = positions[:, None] * frequency[None, :]
    cosine = jnp.cos(angles)
    sine = jnp.sin(angles)
    return jnp.concatenate([cosine, cosine], axis=1), jnp.concatenate([-sine, sine], axis=1)


def kernel(
    n, s_count,
    act_ref, gain_ref, wq_hbm, wk_hbm, wv_hbm, wo_hbm, cache_hbm, post_ref, cos_ref, sin_ref,
    out_ref,
    wq, wk, wv, wo, rows, q_buf, kv, att, slots, acc,
    w_sem, cache_sem, ag_send, ag_recv, kv_send, kv_recv, rs_send, rs_recv,
):
    s = lax.axis_index("seq")
    z = lax.axis_index("head")
    R, D = act_ref.shape
    kv_width = wk.shape[1]
    heads_kv = kv_width // HD
    group = wq.shape[1] // kv_width
    CR = R // ROW_CHUNKS
    CD = D // COL_CHUNKS

    weight_copies = [
        pltpu.make_async_copy(src, dst, w_sem.at[i])
        for i, (src, dst) in enumerate([(wq_hbm, wq), (wk_hbm, wk), (wv_hbm, wv), (wo_hbm, wo)])
    ]
    for c in weight_copies:
        c.start()

    def cache_copies(d):
        return [
            pltpu.make_async_copy(
                cache_hbm.at[i, pl.ds(pl.multiple_of(WINDOW + (s - d) * TOK_DEV, TOK_DEV), TOK_DEV), :],
                kv.at[pl.ds(WINDOW - d * TOK_DEV, TOK_DEV), pl.ds(i * kv_width, kv_width)],
                cache_sem.at[d - 1, i],
            )
            for i in range(2)
        ]

    for d in range(1, REACH + 1):
        @pl.when(s < d)
        def _():
            for c in cache_copies(d):
                c.start()

    barrier = pltpu.get_barrier_semaphore()

    def greet(cond, ds, dz):
        @pl.when(cond)
        def _():
            pl.semaphore_signal(barrier, inc=1, device_id=(s + ds, z + dz), device_id_type=MESH)

    partners = [(z > 0, 0, -1), (z < n - 1, 0, 1)]
    for d in range(1, REACH + 1):
        partners += [(s >= d, -d, 0), (s + d < s_count, d, 0)]
    for p in partners:
        greet(*p)

    def norm_chunk(i, carry):
        r0 = pl.multiple_of(i * 16, 16)
        x = act_ref[pl.ds(r0, 16), :].astype(jnp.float32)
        y = x * lax.rsqrt(jnp.mean(x * x, axis=-1, keepdims=True) + EPSILON) * gain_ref[...]
        rows[z, pl.ds(r0, 16), :] = y.astype(jnp.bfloat16)
        return carry

    lax.fori_loop(0, R // 16, norm_chunk, 0)
    pl.semaphore_wait(barrier, sum(jnp.where(p[0], 1, 0) for p in partners))

    right = lax.rem(z + 1, n)
    left = lax.rem(z + n - 1, n)

    def ag_copy(direction, block, c):
        where = rows.at[block, pl.ds(c * CR, CR), :]
        return pltpu.make_async_remote_copy(
            src_ref=where, dst_ref=where,
            send_sem=ag_send.at[direction, block, c], recv_sem=ag_recv.at[direction, block, c],
            device_id=(s, right if direction == 0 else left), device_id_type=MESH,
        )

    def kv_copy(d, block):
        r0 = pl.multiple_of(block * R, R)
        return pltpu.make_async_remote_copy(
            src_ref=kv.at[pl.ds(WINDOW + r0, R), :],
            dst_ref=kv.at[pl.ds(WINDOW - d * TOK_DEV + r0, R), :],
            send_sem=kv_send.at[d - 1, block], recv_sem=kv_recv.at[d - 1, block],
            device_id=(lax.rem(s + d, s_count), z), device_id_type=MESH,
        )

    def rs_copy(direction, block, slot, c):
        where = slots.at[slot, c]
        return pltpu.make_async_remote_copy(
            src_ref=where, dst_ref=where,
            send_sem=rs_send.at[direction, block, c], recv_sem=rs_recv.at[direction, block, c],
            device_id=(s, right if direction == 0 else left), device_id_type=MESH,
        )

    def project(block):
        r0 = pl.multiple_of(block * R, R)
        cosine = cos_ref[pl.ds(r0, R), :]
        sine = sin_ref[pl.ds(r0, R), :]

        def run(w, tile, rotary, scale, dst, dst_r0, dst_c0):
            def one(i, carry):
                c0 = pl.multiple_of(i * tile, tile)
                t = jnp.dot(rows[block], w[:, pl.ds(c0, tile)], preferred_element_type=jnp.float32)
                for h in range(tile // HD):
                    u = t[:, h * HD:(h + 1) * HD]
                    if rotary:
                        u = u * cosine + pltpu.roll(u, HD // 2, 1) * sine
                    if scale is not None:
                        u = u * scale
                    dst[pl.ds(dst_r0, R), pl.ds(pl.multiple_of(dst_c0 + c0 + h * HD, HD), HD)] = u.astype(jnp.bfloat16)
                return carry
            lax.fori_loop(0, w.shape[1] // tile, one, 0)

        tile = min(256, kv_width)
        own = pl.multiple_of(WINDOW + r0, R)
        run(wk, tile, True, None, kv, own, 0)
        run(wv, tile, False, None, kv, own, kv_width)
        for d in range(1, REACH + 1):
            @pl.when(s + d < s_count)
            def _():
                kv_copy(d, block).start()
        run(wq, 256, True, SCALAR ** (-0.5), q_buf, r0, 0)

    def first_sends(direction, cond):
        @pl.when(cond)
        def _():
            for c in range(ROW_CHUNKS):
                ag_copy(direction, z, c).start()

    first_sends(0, z < n - 1)
    first_sends(1, z > 0)
    for i in (1, 2, 0):
        weight_copies[i].wait()
    project(z)

    def gather_step(t, carry):
        from_left = z - t
        from_right = z + t
        for c in range(ROW_CHUNKS):
            @pl.when(from_left >= 0)
            def _():
                ag_copy(0, from_left, c).wait_recv()

                @pl.when(z < n - 1)
                def _():
                    ag_copy(0, from_left, c).start()

            @pl.when(from_right < n)
            def _():
                ag_copy(1, from_right, c).wait_recv()

                @pl.when(z > 0)
                def _():
                    ag_copy(1, from_right, c).start()

        @pl.when(from_left >= 0)
        def _():
            project(from_left)

        @pl.when(from_right < n)
        def _():
            project(from_right)
        return carry

    lax.fori_loop(1, n, gather_step, 0)

    for d in range(1, REACH + 1):
        @pl.when(s < d)
        def _():
            for c in cache_copies(d):
                c.wait()

        @pl.when(s >= d)
        def _():
            lax.fori_loop(0, n, lambda b, carry: (kv_copy(d, b).wait_recv(), carry)[1], 0)
    weight_copies[3].wait()

    row_i = lax.broadcasted_iota(jnp.int32, (group * R, R), 0)
    row_i = lax.rem(row_i, R)
    col_i = lax.broadcasted_iota(jnp.int32, (group * R, R), 1)
    later = col_i > row_i
    spans = [(0, R), (R, WINDOW - R), (WINDOW, R)]

    def attend(block):
        r0 = pl.multiple_of(block * R, R)
        for g in range(heads_kv):
            q = jnp.concatenate(
                [q_buf[pl.ds(r0, R), (g * group + a) * HD:(g * group + a + 1) * HD] for a in range(group)], axis=0
            )
            scores = []
            for j, (o, w) in enumerate(spans):
                k = kv[pl.ds(pl.multiple_of(r0 + o, R), w), g * HD:(g + 1) * HD]
                sc = lax.dot_general(q, k, (((1,), (1,)), ((), ())), preferred_element_type=jnp.float32)
                if j == 0:
                    sc = jnp.where(later, sc, -jnp.inf)
                if j == 2:
                    sc = jnp.where(later, -jnp.inf, sc)
                scores.append(sc)
            m = functools.reduce(jnp.maximum, [jnp.max(x, axis=-1, keepdims=True) for x in scores])
            total = 0.0
            o_sum = 0.0
            for (o, w), sc in zip(spans, scores):
                e = jnp.exp(sc - m)
                total = total + jnp.sum(e, axis=-1, keepdims=True)
                v = kv[pl.ds(pl.multiple_of(r0 + o, R), w), kv_width + g * HD:kv_width + (g + 1) * HD]
                o_sum = o_sum + jnp.dot(e.astype(jnp.bfloat16), v, preferred_element_type=jnp.float32)
            o_sum = (o_sum / total).astype(jnp.bfloat16)
            for a in range(group):
                att[:, (g * group + a) * HD:(g * group + a + 1) * HD] = o_sum[a * R:(a + 1) * R]

    TILE = 256

    def partial_out(direction, block, incoming):
        attend(block)
        for c in range(COL_CHUNKS):
            @pl.when(incoming)
            def _():
                rs_copy(direction, block, block, c).wait_recv()

            def one(i, carry):
                c0 = pl.multiple_of(i * TILE, TILE)
                w0 = pl.multiple_of(c * CD + i * TILE, TILE)
                p = jnp.dot(att[...], wo[:, pl.ds(w0, TILE)], preferred_element_type=jnp.float32)
                before = slots[block, c, :, pl.ds(c0, TILE)].astype(jnp.float32)
                p = p + jnp.where(incoming, before, 0.0)
                slots[block, c, :, pl.ds(c0, TILE)] = p.astype(jnp.bfloat16)
                return carry
            lax.fori_loop(0, CD // TILE, one, 0)
            send_out(direction, block, c).start()

    def send_out(direction, block, c):
        if direction == 0:
            return rs_copy(0, block, block, c)
        last = jnp.where(block == z - 1, n, block)
        return pltpu.make_async_remote_copy(
            src_ref=slots.at[block, c], dst_ref=slots.at[last, c],
            send_sem=rs_send.at[1, block, c], recv_sem=rs_recv.at[1, block, c],
            device_id=(s, left), device_id_type=MESH,
        )

    def scatter_step(t, carry):
        to_right = n - t
        to_left = t - 1

        @pl.when(to_right > z)
        def _():
            partial_out(0, to_right, z > 0)

        @pl.when(to_left < z)
        def _():
            partial_out(1, to_left, z < n - 1)
        return carry

    lax.fori_loop(1, n, scatter_step, 0)

    attend(z)

    def own(i, carry):
        w0 = pl.multiple_of(i * TILE, TILE)
        acc[:, pl.ds(w0, TILE)] = jnp.dot(att[...], wo[:, pl.ds(w0, TILE)], preferred_element_type=jnp.float32)
        return carry
    lax.fori_loop(0, D // TILE, own, 0)

    for c in range(COL_CHUNKS):
        for direction, slot, cond in ((0, z, z > 0), (1, n, z < n - 1)):
            @pl.when(cond)
            def _():
                rs_copy(direction, z, slot, c).wait_recv()
                acc[:, c * CD:(c + 1) * CD] += slots[slot, c].astype(jnp.float32)

    def finish(i, carry):
        r0 = pl.multiple_of(i * 16, 16)
        x = acc[pl.ds(r0, 16), :]
        y = x * lax.rsqrt(jnp.mean(x * x, axis=-1, keepdims=True) + EPSILON) * post_ref[...]
        out_ref[pl.ds(r0, 16), :] = (act_ref[pl.ds(r0, 16), :].astype(jnp.float32) + y).astype(jnp.bfloat16)
        return carry
    lax.fori_loop(0, R // 16, finish, 0)

    def drain(b, carry):
        @pl.when((b <= z) & (z < n - 1))
        def _():
            for c in range(ROW_CHUNKS):
                ag_copy(0, b, c).wait_send()

        @pl.when((b >= z) & (z > 0))
        def _():
            for c in range(ROW_CHUNKS):
                ag_copy(1, b, c).wait_send()

        @pl.when(b > z)
        def _():
            for c in range(COL_CHUNKS):
                send_out(0, b, c).wait_send()

        @pl.when(b < z)
        def _():
            for c in range(COL_CHUNKS):
                send_out(1, b, c).wait_send()

        for d in range(1, REACH + 1):
            @pl.when(s + d < s_count)
            def _():
                kv_copy(d, b).wait_send()
        return carry
    lax.fori_loop(0, n, drain, 0)


def per_device(n, s_count, act, gain, wq, wk, wv, wo, cache, post):
    R, D = act.shape
    s = lax.axis_index("seq")
    positions = (s * TOK_DEV + jnp.arange(TOK_DEV, dtype=jnp.int32)).astype(jnp.float32)
    cosine, sine = rope_tables(positions)
    bf, f32 = jnp.bfloat16, jnp.float32
    vmem = pl.BlockSpec(memory_space=pltpu.VMEM)
    hbm = pl.BlockSpec(memory_space=pl.ANY)
    dma = pltpu.SemaphoreType.DMA
    return pl.pallas_call(
        functools.partial(kernel, n, s_count),
        out_shape=jax.ShapeDtypeStruct((R, D), bf),
        in_specs=[vmem, vmem, hbm, hbm, hbm, hbm, hbm, vmem, vmem, vmem],
        out_specs=vmem,
        scratch_shapes=[
            pltpu.VMEM(wq.shape, bf),
            pltpu.VMEM(wk.shape, bf),
            pltpu.VMEM(wv.shape, bf),
            pltpu.VMEM(wo.shape, bf),
            pltpu.VMEM((n, R, D), bf),
            pltpu.VMEM((TOK_DEV, wq.shape[1]), bf),
            pltpu.VMEM((WINDOW + TOK_DEV, 2 * wk.shape[1]), bf),
            pltpu.VMEM((R, wo.shape[0]), bf),
            pltpu.VMEM((n + 1, COL_CHUNKS, R, D // COL_CHUNKS), bf),
            pltpu.VMEM((R, D), f32),
            dma((4,)),
            dma((REACH, 2)),
            dma((2, n, ROW_CHUNKS)),
            dma((2, n, ROW_CHUNKS)),
            dma((REACH, n)),
            dma((REACH, n)),
            dma((2, n, COL_CHUNKS)),
            dma((2, n, COL_CHUNKS)),
        ],
        compiler_params=pltpu.CompilerParams(
            collective_id=0, has_side_effects=True, vmem_limit_bytes=62 * 1024 * 1024
        ),
    )(act, gain.reshape(1, -1), wq, wk, wv, wo, cache, post.reshape(1, -1), cosine, sine)


def solution(mesh):
    return jax.shard_map(
        functools.partial(per_device, mesh.shape["head"], mesh.shape["seq"]),
        mesh=mesh,
        in_specs=(
            P(("seq", "head"), None),
            P(),
            P(None, "head"),
            P(None, "head"),
            P(None, "head"),
            P("head", None),
            P(None, None, "head"),
            P(),
        ),
        out_specs=P(("seq", "head"), None),
        check_vma=False,
    )
```

```python
import functools
import jax
import jax.numpy as jnp
from jax import lax
from jax.experimental import pallas as pl
from jax.experimental.pallas import tpu as pltpu
from jax.sharding import PartitionSpec as P

HD = 128
WINDOW = 1024
SCALAR = 168
TOK_DEV = 512
EPSILON = 1e-06
ROPE_BASE = 10000.0
REACH = WINDOW // TOK_DEV
COL_CHUNKS = 3
MESH = pl.DeviceIdType.MESH


def rope_tables(positions):
    half_size = HD // 2
    frequency = ROPE_BASE ** (-(jnp.arange(half_size, dtype=jnp.float32) * 2.0 / HD))
    angles = positions[:, None] * frequency[None, :]
    cosine = jnp.cos(angles)
    sine = jnp.sin(angles)
    return jnp.concatenate([cosine, cosine], axis=1), jnp.concatenate([-sine, sine], axis=1)


def kernel(
    n, s_count,
    act_ref, gain_ref, wq_hbm, wk_hbm, wv_hbm, wo_hbm, cache_hbm, post_ref, cos_ref, sin_ref,
    out_ref,
    wq, wk, wv, wo, rows, q_buf, kv, att, slots, acc,
    w_sem, cache_sem, ag_send, ag_recv, kv_send, kv_recv, rs_send, rs_recv,
):
    s = lax.axis_index("seq")
    z = lax.axis_index("head")
    R, D = act_ref.shape
    kv_width = wk.shape[1]
    heads_kv = kv_width // HD
    group = wq.shape[1] // kv_width
    row_chunks = ag_send.shape[2]
    CR = R // row_chunks
    CD = D // COL_CHUNKS

    weight_copies = [
        pltpu.make_async_copy(src, dst, w_sem.at[i])
        for i, (src, dst) in enumerate([(wq_hbm, wq), (wk_hbm, wk), (wv_hbm, wv), (wo_hbm, wo)])
    ]
    for c in weight_copies:
        c.start()

    def cache_copies(d):
        return [
            pltpu.make_async_copy(
                cache_hbm.at[i, pl.ds(pl.multiple_of(WINDOW + (s - d) * TOK_DEV, TOK_DEV), TOK_DEV), :],
                kv.at[pl.ds(WINDOW - d * TOK_DEV, TOK_DEV), pl.ds(i * kv_width, kv_width)],
                cache_sem.at[d - 1, i],
            )
            for i in range(2)
        ]

    for d in range(1, REACH + 1):
        @pl.when(s < d)
        def _():
            for c in cache_copies(d):
                c.start()

    barrier = pltpu.get_barrier_semaphore()

    def greet(cond, ds, dz):
        @pl.when(cond)
        def _():
            pl.semaphore_signal(barrier, inc=1, device_id=(s + ds, z + dz), device_id_type=MESH)

    partners = [(z > 0, 0, -1), (z < n - 1, 0, 1)]
    for d in range(1, REACH + 1):
        partners += [(s >= d, -d, 0), (s + d < s_count, d, 0)]
    for p in partners:
        greet(*p)

    def norm_chunk(i, carry):
        r0 = pl.multiple_of(i * 16, 16)
        x = act_ref[pl.ds(r0, 16), :].astype(jnp.float32)
        y = x * lax.rsqrt(jnp.mean(x * x, axis=-1, keepdims=True) + EPSILON) * gain_ref[...].reshape(1, D)
        rows[z, pl.ds(r0, 16), :] = y.astype(jnp.bfloat16)
        return carry

    lax.fori_loop(0, R // 16, norm_chunk, 0)
    pl.semaphore_wait(barrier, sum(jnp.where(p[0], 1, 0) for p in partners))

    right = lax.rem(z + 1, n)
    left = lax.rem(z + n - 1, n)

    def ag_copy(direction, block, c):
        where = rows.at[block, pl.ds(c * CR, CR), :]
        return pltpu.make_async_remote_copy(
            src_ref=where, dst_ref=where,
            send_sem=ag_send.at[direction, block, c], recv_sem=ag_recv.at[direction, block, c],
            device_id=(s, right if direction == 0 else left), device_id_type=MESH,
        )

    def kv_copy(d, block):
        r0 = pl.multiple_of(block * R, R)
        return pltpu.make_async_remote_copy(
            src_ref=kv.at[pl.ds(WINDOW + r0, R), :],
            dst_ref=kv.at[pl.ds(WINDOW - d * TOK_DEV + r0, R), :],
            send_sem=kv_send.at[d - 1, block], recv_sem=kv_recv.at[d - 1, block],
            device_id=(lax.rem(s + d, s_count), z), device_id_type=MESH,
        )

    def rs_copy(direction, block, slot, c):
        where = slots.at[slot, c]
        return pltpu.make_async_remote_copy(
            src_ref=where, dst_ref=where,
            send_sem=rs_send.at[direction, block, c], recv_sem=rs_recv.at[direction, block, c],
            device_id=(s, right if direction == 0 else left), device_id_type=MESH,
        )

    def project(block):
        r0 = pl.multiple_of(block * R, R)
        cosine = cos_ref[pl.ds(r0, R), :]
        sine = sin_ref[pl.ds(r0, R), :]

        def run(w, tile, rotary, scale, dst, dst_r0, dst_c0):
            def one(i, carry):
                c0 = pl.multiple_of(i * tile, tile)
                t = jnp.dot(rows[block], w[:, pl.ds(c0, tile)], preferred_element_type=jnp.float32)
                for h in range(tile // HD):
                    u = t[:, h * HD:(h + 1) * HD]
                    if rotary:
                        u = u * cosine + pltpu.roll(u, HD // 2, 1) * sine
                    if scale is not None:
                        u = u * scale
                    dst[pl.ds(dst_r0, R), pl.ds(pl.multiple_of(dst_c0 + c0 + h * HD, HD), HD)] = u.astype(jnp.bfloat16)
                return carry
            lax.fori_loop(0, w.shape[1] // tile, one, 0)

        tile = min(256, kv_width)
        own = pl.multiple_of(WINDOW + r0, R)
        run(wk, tile, True, None, kv, own, 0)
        run(wv, tile, False, None, kv, own, kv_width)
        for d in range(1, REACH + 1):
            @pl.when(s + d < s_count)
            def _():
                kv_copy(d, block).start()
        run(wq, 256, True, SCALAR ** (-0.5), q_buf, r0, 0)

    def first_sends(direction, cond):
        @pl.when(cond)
        def _():
            for c in range(row_chunks):
                ag_copy(direction, z, c).start()

    first_sends(0, z < n - 1)
    first_sends(1, z > 0)
    for i in (1, 2, 0):
        weight_copies[i].wait()
    def gather_step(t, carry):
        from_left = z - t
        from_right = z + t
        for c in range(row_chunks):
            @pl.when(from_left >= 0)
            def _():
                ag_copy(0, from_left, c).wait_recv()

                @pl.when(z < n - 1)
                def _():
                    ag_copy(0, from_left, c).start()

            @pl.when(from_right < n)
            def _():
                ag_copy(1, from_right, c).wait_recv()

                @pl.when(z > 0)
                def _():
                    ag_copy(1, from_right, c).start()

            if c == 0:
                @pl.when(from_right - 1 < n)
                def _():
                    project(from_right - 1)

        @pl.when(from_left >= 0)
        def _():
            project(from_left)
        return carry

    lax.fori_loop(1, n, gather_step, 0)

    @pl.when(z == 0)
    def _():
        project(n - 1)

    for d in range(1, REACH + 1):
        @pl.when(s < d)
        def _():
            for c in cache_copies(d):
                c.wait()

        @pl.when(s >= d)
        def _():
            lax.fori_loop(0, n, lambda b, carry: (kv_copy(d, b).wait_recv(), carry)[1], 0)
    weight_copies[3].wait()

    row_i = lax.broadcasted_iota(jnp.int32, (group * R, R), 0)
    row_i = lax.rem(row_i, R)
    col_i = lax.broadcasted_iota(jnp.int32, (group * R, R), 1)
    later = col_i > row_i
    spans = [(0, R), (R, WINDOW - R), (WINDOW, R)]

    def attend(block):
        r0 = pl.multiple_of(block * R, R)
        for g in range(heads_kv):
            q = jnp.concatenate(
                [q_buf[pl.ds(r0, R), (g * group + a) * HD:(g * group + a + 1) * HD] for a in range(group)], axis=0
            )
            scores = []
            for j, (o, w) in enumerate(spans):
                k = kv[pl.ds(pl.multiple_of(r0 + o, R), w), g * HD:(g + 1) * HD]
                sc = lax.dot_general(q, k, (((1,), (1,)), ((), ())), preferred_element_type=jnp.float32)
                if j == 0:
                    sc = jnp.where(later, sc, -jnp.inf)
                if j == 2:
                    sc = jnp.where(later, -jnp.inf, sc)
                scores.append(sc)
            m = functools.reduce(jnp.maximum, [jnp.max(x, axis=-1, keepdims=True) for x in scores])
            total = 0.0
            o_sum = 0.0
            for (o, w), sc in zip(spans, scores):
                e = jnp.exp(sc - m)
                total = total + jnp.sum(e, axis=-1, keepdims=True)
                v = kv[pl.ds(pl.multiple_of(r0 + o, R), w), kv_width + g * HD:kv_width + (g + 1) * HD]
                o_sum = o_sum + jnp.dot(e.astype(jnp.bfloat16), v, preferred_element_type=jnp.float32)
            o_sum = (o_sum / total).astype(jnp.bfloat16)
            for a in range(group):
                att[:, (g * group + a) * HD:(g * group + a + 1) * HD] = o_sum[a * R:(a + 1) * R]

    TILE = 256

    def partial_out(direction, block, incoming):
        attend(block)
        for c in range(COL_CHUNKS):
            @pl.when(incoming)
            def _():
                rs_copy(direction, block, block, c).wait_recv()

            def one(i, carry):
                c0 = pl.multiple_of(i * TILE, TILE)
                w0 = pl.multiple_of(c * CD + i * TILE, TILE)
                p = jnp.dot(att[...], wo[:, pl.ds(w0, TILE)], preferred_element_type=jnp.float32)
                before = slots[block, c, :, pl.ds(c0, TILE)].astype(jnp.float32)
                p = p + jnp.where(incoming, before, 0.0)
                slots[block, c, :, pl.ds(c0, TILE)] = p.astype(jnp.bfloat16)
                return carry
            lax.fori_loop(0, CD // TILE, one, 0)
            send_out(direction, block, c).start()

    def send_out(direction, block, c):
        if direction == 0:
            return rs_copy(0, block, block, c)
        last = jnp.where(block == z - 1, n, block)
        return pltpu.make_async_remote_copy(
            src_ref=slots.at[block, c], dst_ref=slots.at[last, c],
            send_sem=rs_send.at[1, block, c], recv_sem=rs_recv.at[1, block, c],
            device_id=(s, left), device_id_type=MESH,
        )

    def scatter_step(t, carry):
        to_right = n - t
        to_left = t - 1

        @pl.when(to_right > z)
        def _():
            partial_out(0, to_right, z > 0)

        @pl.when(to_left < z)
        def _():
            partial_out(1, to_left, z < n - 1)
        return carry

    lax.fori_loop(1, n, scatter_step, 0)

    attend(z)

    def own(i, carry):
        w0 = pl.multiple_of(i * TILE, TILE)
        acc[:, pl.ds(w0, TILE)] = jnp.dot(att[...], wo[:, pl.ds(w0, TILE)], preferred_element_type=jnp.float32)
        return carry
    lax.fori_loop(0, D // TILE, own, 0)

    for c in range(COL_CHUNKS):
        for direction, slot, cond in ((0, z, z > 0), (1, n, z < n - 1)):
            @pl.when(cond)
            def _():
                rs_copy(direction, z, slot, c).wait_recv()
                acc[:, c * CD:(c + 1) * CD] += slots[slot, c].astype(jnp.float32)

    def finish(i, carry):
        r0 = pl.multiple_of(i * 16, 16)
        x = acc[pl.ds(r0, 16), :]
        y = x * lax.rsqrt(jnp.mean(x * x, axis=-1, keepdims=True) + EPSILON) * post_ref[...].reshape(1, D)
        out_ref[pl.ds(r0, 16), :] = (act_ref[pl.ds(r0, 16), :].astype(jnp.float32) + y).astype(jnp.bfloat16)
        return carry
    lax.fori_loop(0, R // 16, finish, 0)

    def drain(b, carry):
        @pl.when((b <= z) & (z < n - 1))
        def _():
            for c in range(row_chunks):
                ag_copy(0, b, c).wait_send()

        @pl.when((b >= z) & (z > 0))
        def _():
            for c in range(row_chunks):
                ag_copy(1, b, c).wait_send()

        @pl.when(b > z)
        def _():
            for c in range(COL_CHUNKS):
                send_out(0, b, c).wait_send()

        @pl.when(b < z)
        def _():
            for c in range(COL_CHUNKS):
                send_out(1, b, c).wait_send()

        for d in range(1, REACH + 1):
            @pl.when(s + d < s_count)
            def _():
                kv_copy(d, b).wait_send()
        return carry
    lax.fori_loop(0, n, drain, 0)


def per_device(n, s_count, act, gain, wq, wk, wv, wo, cache, post):
    R, D = act.shape
    row_chunks = min(2, R // 16)
    s = lax.axis_index("seq")
    positions = (s * TOK_DEV + jnp.arange(TOK_DEV, dtype=jnp.int32)).astype(jnp.float32)
    cosine, sine = rope_tables(positions)
    bf, f32 = jnp.bfloat16, jnp.float32
    vmem = pl.BlockSpec(memory_space=pltpu.VMEM)
    hbm = pl.BlockSpec(memory_space=pl.ANY)
    dma = pltpu.SemaphoreType.DMA
    return pl.pallas_call(
        functools.partial(kernel, n, s_count),
        out_shape=jax.ShapeDtypeStruct((R, D), bf),
        in_specs=[vmem, vmem, hbm, hbm, hbm, hbm, hbm, vmem, vmem, vmem],
        out_specs=vmem,
        scratch_shapes=[
            pltpu.VMEM(wq.shape, bf),
            pltpu.VMEM(wk.shape, bf),
            pltpu.VMEM(wv.shape, bf),
            pltpu.VMEM(wo.shape, bf),
            pltpu.VMEM((n, R, D), bf),
            pltpu.VMEM((TOK_DEV, wq.shape[1]), bf),
            pltpu.VMEM((WINDOW + TOK_DEV, 2 * wk.shape[1]), bf),
            pltpu.VMEM((R, wo.shape[0]), bf),
            pltpu.VMEM((n + 1, COL_CHUNKS, R, D // COL_CHUNKS), bf),
            pltpu.VMEM((R, D), f32),
            dma((4,)),
            dma((REACH, 2)),
            dma((2, n, row_chunks)),
            dma((2, n, row_chunks)),
            dma((REACH, n)),
            dma((REACH, n)),
            dma((2, n, COL_CHUNKS)),
            dma((2, n, COL_CHUNKS)),
        ],
        compiler_params=pltpu.CompilerParams(
            collective_id=0, has_side_effects=True, vmem_limit_bytes=62 * 1024 * 1024
        ),
    )(act, gain, wq, wk, wv, wo, cache, post, cosine, sine)


def solution(mesh):
    return jax.shard_map(
        functools.partial(per_device, mesh.shape["head"], mesh.shape["seq"]),
        mesh=mesh,
        in_specs=(
            P(("seq", "head"), None),
            P(),
            P(None, "head"),
            P(None, "head"),
            P(None, "head"),
            P("head", None),
            P(None, None, "head"),
            P(),
        ),
        out_specs=P(("seq", "head"), None),
        check_vma=False,
    )
```

```python
import functools
import jax
import jax.numpy as jnp
from jax import lax
from jax.experimental import pallas as pl
from jax.experimental.pallas import tpu as pltpu
from jax.sharding import PartitionSpec as P

HD = 128
WINDOW = 1024
SCALAR = 168
TOK_DEV = 512
EPSILON = 1e-06
ROPE_BASE = 10000.0
REACH = WINDOW // TOK_DEV
COL_CHUNKS = 7
MESH = pl.DeviceIdType.MESH


def rope_tables(positions):
    half_size = HD // 2
    frequency = ROPE_BASE ** (-(jnp.arange(half_size, dtype=jnp.float32) * 2.0 / HD))
    angles = positions[:, None] * frequency[None, :]
    cosine = jnp.cos(angles)
    sine = jnp.sin(angles)
    return jnp.concatenate([cosine, cosine], axis=1), jnp.concatenate([-sine, sine], axis=1)


def kernel(
    n, s_count,
    act_ref, gain_ref, wq_hbm, wk_hbm, wv_hbm, wo_hbm, cache_hbm, post_ref, cos_ref, sin_ref,
    out_ref,
    wq, wk, wv, wo, rows, q_buf, kv, att, slots, acc,
    w_sem, cache_sem, ag_send, ag_recv, kv_send, kv_recv, rs_send, rs_recv,
):
    s = lax.axis_index("seq")
    z = lax.axis_index("head")
    R, D = act_ref.shape
    kv_width = wk.shape[1]
    heads_kv = kv_width // HD
    group = wq.shape[1] // kv_width
    row_chunks = ag_send.shape[2]
    CR = R // row_chunks
    CD = D // COL_CHUNKS

    weight_copies = [
        pltpu.make_async_copy(src, dst, w_sem.at[i])
        for i, (src, dst) in enumerate([(wk_hbm, wk), (wv_hbm, wv), (wq_hbm, wq), (wo_hbm, wo)])
    ]
    for c in weight_copies:
        c.start()

    def cache_copies(d):
        return [
            pltpu.make_async_copy(
                cache_hbm.at[i, pl.ds(pl.multiple_of(WINDOW + (s - d) * TOK_DEV, TOK_DEV), TOK_DEV), :],
                kv.at[pl.ds(WINDOW - d * TOK_DEV, TOK_DEV), pl.ds(i * kv_width, kv_width)],
                cache_sem.at[d - 1, i],
            )
            for i in range(2)
        ]

    for d in range(1, REACH + 1):
        @pl.when(s < d)
        def _():
            for c in cache_copies(d):
                c.start()

    barrier = pltpu.get_barrier_semaphore()

    def greet(cond, ds, dz):
        @pl.when(cond)
        def _():
            pl.semaphore_signal(barrier, inc=1, device_id=(s + ds, z + dz), device_id_type=MESH)

    partners = [(z > 0, 0, -1), (z < n - 1, 0, 1)]
    for d in range(1, REACH + 1):
        partners += [(s >= d, -d, 0), (s + d < s_count, d, 0)]
    for p in partners:
        greet(*p)

    def norm_chunk(i, carry):
        r0 = pl.multiple_of(i * 16, 16)
        x = act_ref[pl.ds(r0, 16), :].astype(jnp.float32)
        y = x * lax.rsqrt(jnp.mean(x * x, axis=-1, keepdims=True) + EPSILON) * gain_ref[...].reshape(1, D)
        rows[z, pl.ds(r0, 16), :] = y.astype(jnp.bfloat16)
        return carry

    pl.semaphore_wait(barrier, sum(jnp.where(p[0], 1, 0) for p in partners))

    right = lax.rem(z + 1, n)
    left = lax.rem(z + n - 1, n)

    def ag_copy(direction, block, c):
        where = rows.at[block, pl.ds(c * CR, CR), :]
        return pltpu.make_async_remote_copy(
            src_ref=where, dst_ref=where,
            send_sem=ag_send.at[direction, block, c], recv_sem=ag_recv.at[direction, block, c],
            device_id=(s, right if direction == 0 else left), device_id_type=MESH,
        )

    def kv_copy(d, block):
        r0 = pl.multiple_of(block * R, R)
        return pltpu.make_async_remote_copy(
            src_ref=kv.at[pl.ds(WINDOW + r0, R), :],
            dst_ref=kv.at[pl.ds(WINDOW - d * TOK_DEV + r0, R), :],
            send_sem=kv_send.at[d - 1, block], recv_sem=kv_recv.at[d - 1, block],
            device_id=(lax.rem(s + d, s_count), z), device_id_type=MESH,
        )

    def rs_copy(direction, block, slot, c):
        where = slots.at[slot, c]
        return pltpu.make_async_remote_copy(
            src_ref=where, dst_ref=where,
            send_sem=rs_send.at[direction, block, c], recv_sem=rs_recv.at[direction, block, c],
            device_id=(s, right if direction == 0 else left), device_id_type=MESH,
        )

    def project(block):
        r0 = pl.multiple_of(block * R, R)
        cosine = cos_ref[pl.ds(r0, R), :]
        sine = sin_ref[pl.ds(r0, R), :]

        def run(w, tile, rotary, scale, dst, dst_r0, dst_c0):
            def one(i, carry):
                c0 = pl.multiple_of(i * tile, tile)
                t = jnp.dot(rows[block], w[:, pl.ds(c0, tile)], preferred_element_type=jnp.float32)
                for h in range(tile // HD):
                    u = t[:, h * HD:(h + 1) * HD]
                    if rotary:
                        u = u * cosine + pltpu.roll(u, HD // 2, 1) * sine
                    if scale is not None:
                        u = u * scale
                    dst[pl.ds(dst_r0, R), pl.ds(pl.multiple_of(dst_c0 + c0 + h * HD, HD), HD)] = u.astype(jnp.bfloat16)
                return carry
            lax.fori_loop(0, w.shape[1] // tile, one, 0)

        tile = min(256, kv_width)
        own = pl.multiple_of(WINDOW + r0, R)
        run(wk, tile, True, None, kv, own, 0)
        run(wv, tile, False, None, kv, own, kv_width)
        for d in range(1, REACH + 1):
            @pl.when(s + d < s_count)
            def _():
                kv_copy(d, block).start()
        run(wq, 256, True, SCALAR ** (-0.5), q_buf, r0, 0)

    for c in range(row_chunks):
        lax.fori_loop(c * CR // 16, (c + 1) * CR // 16, norm_chunk, 0)

        @pl.when(z < n - 1)
        def _():
            ag_copy(0, z, c).start()

        @pl.when(z > 0)
        def _():
            ag_copy(1, z, c).start()

    for i in range(3):
        weight_copies[i].wait()
    def gather_step(t, carry):
        from_left = z - t
        from_right = z + t
        for c in range(row_chunks):
            @pl.when(from_left >= 0)
            def _():
                ag_copy(0, from_left, c).wait_recv()

                @pl.when(z < n - 1)
                def _():
                    ag_copy(0, from_left, c).start()

            @pl.when(from_right < n)
            def _():
                ag_copy(1, from_right, c).wait_recv()

                @pl.when(z > 0)
                def _():
                    ag_copy(1, from_right, c).start()

            if c == 0:
                @pl.when(from_right - 1 < n)
                def _():
                    project(from_right - 1)

        @pl.when(from_left >= 0)
        def _():
            project(from_left)
        return carry

    lax.fori_loop(1, n, gather_step, 0)

    @pl.when(z == 0)
    def _():
        project(n - 1)

    for d in range(1, REACH + 1):
        @pl.when(s < d)
        def _():
            for c in cache_copies(d):
                c.wait()

        @pl.when(s >= d)
        def _():
            lax.fori_loop(0, n, lambda b, carry: (kv_copy(d, b).wait_recv(), carry)[1], 0)
    weight_copies[3].wait()

    row_i = lax.broadcasted_iota(jnp.int32, (group * R, R), 0)
    row_i = lax.rem(row_i, R)
    col_i = lax.broadcasted_iota(jnp.int32, (group * R, R), 1)
    later = col_i > row_i
    spans = [(0, R), (R, WINDOW - R), (WINDOW, R)]

    def attend(block):
        r0 = pl.multiple_of(block * R, R)
        for g in range(heads_kv):
            q = jnp.concatenate(
                [q_buf[pl.ds(r0, R), (g * group + a) * HD:(g * group + a + 1) * HD] for a in range(group)], axis=0
            )
            scores = []
            for j, (o, w) in enumerate(spans):
                k = kv[pl.ds(pl.multiple_of(r0 + o, R), w), g * HD:(g + 1) * HD]
                sc = lax.dot_general(q, k, (((1,), (1,)), ((), ())), preferred_element_type=jnp.float32)
                if j == 0:
                    sc = jnp.where(later, sc, -jnp.inf)
                if j == 2:
                    sc = jnp.where(later, -jnp.inf, sc)
                scores.append(sc)
            m = functools.reduce(jnp.maximum, [jnp.max(x, axis=-1, keepdims=True) for x in scores])
            total = 0.0
            o_sum = 0.0
            for (o, w), sc in zip(spans, scores):
                e = jnp.exp(sc - m)
                total = total + jnp.sum(e, axis=-1, keepdims=True)
                v = kv[pl.ds(pl.multiple_of(r0 + o, R), w), kv_width + g * HD:kv_width + (g + 1) * HD]
                o_sum = o_sum + jnp.dot(e.astype(jnp.bfloat16), v, preferred_element_type=jnp.float32)
            o_sum = (o_sum / total).astype(jnp.bfloat16)
            for a in range(group):
                att[:, (g * group + a) * HD:(g * group + a + 1) * HD] = o_sum[a * R:(a + 1) * R]

    TILE = 256

    def partial_out(direction, block, incoming):
        attend(block)
        for c in range(COL_CHUNKS):
            @pl.when(incoming)
            def _():
                rs_copy(direction, block, block, c).wait_recv()

            def one(i, carry):
                c0 = pl.multiple_of(i * TILE, TILE)
                w0 = pl.multiple_of(c * CD + i * TILE, TILE)
                p = jnp.dot(att[...], wo[:, pl.ds(w0, TILE)], preferred_element_type=jnp.float32)
                before = slots[block, c, :, pl.ds(c0, TILE)].astype(jnp.float32)
                p = p + jnp.where(incoming, before, 0.0)
                slots[block, c, :, pl.ds(c0, TILE)] = p.astype(jnp.bfloat16)
                return carry
            lax.fori_loop(0, CD // TILE, one, 0)
            send_out(direction, block, c).start()

    def send_out(direction, block, c):
        if direction == 0:
            return rs_copy(0, block, block, c)
        last = jnp.where(block == z - 1, n, block)
        return pltpu.make_async_remote_copy(
            src_ref=slots.at[block, c], dst_ref=slots.at[last, c],
            send_sem=rs_send.at[1, block, c], recv_sem=rs_recv.at[1, block, c],
            device_id=(s, left), device_id_type=MESH,
        )

    def scatter_step(t, carry):
        to_right = n - t
        to_left = t - 1

        @pl.when(to_right > z)
        def _():
            partial_out(0, to_right, z > 0)

        @pl.when(to_left < z)
        def _():
            partial_out(1, to_left, z < n - 1)
        return carry

    lax.fori_loop(1, n, scatter_step, 0)

    attend(z)

    def own(i, carry):
        w0 = pl.multiple_of(i * TILE, TILE)
        acc[:, pl.ds(w0, TILE)] = jnp.dot(att[...], wo[:, pl.ds(w0, TILE)], preferred_element_type=jnp.float32)
        return carry
    lax.fori_loop(0, D // TILE, own, 0)

    for c in range(COL_CHUNKS):
        for direction, slot, cond in ((0, z, z > 0), (1, n, z < n - 1)):
            @pl.when(cond)
            def _():
                rs_copy(direction, z, slot, c).wait_recv()
                acc[:, c * CD:(c + 1) * CD] += slots[slot, c].astype(jnp.float32)

    def finish(i, carry):
        r0 = pl.multiple_of(i * 16, 16)
        x = acc[pl.ds(r0, 16), :]
        y = x * lax.rsqrt(jnp.mean(x * x, axis=-1, keepdims=True) + EPSILON) * post_ref[...].reshape(1, D)
        out_ref[pl.ds(r0, 16), :] = (act_ref[pl.ds(r0, 16), :].astype(jnp.float32) + y).astype(jnp.bfloat16)
        return carry
    lax.fori_loop(0, R // 16, finish, 0)

    def drain(b, carry):
        @pl.when((b <= z) & (z < n - 1))
        def _():
            for c in range(row_chunks):
                ag_copy(0, b, c).wait_send()

        @pl.when((b >= z) & (z > 0))
        def _():
            for c in range(row_chunks):
                ag_copy(1, b, c).wait_send()

        @pl.when(b > z)
        def _():
            for c in range(COL_CHUNKS):
                send_out(0, b, c).wait_send()

        @pl.when(b < z)
        def _():
            for c in range(COL_CHUNKS):
                send_out(1, b, c).wait_send()

        for d in range(1, REACH + 1):
            @pl.when(s + d < s_count)
            def _():
                kv_copy(d, b).wait_send()
        return carry
    lax.fori_loop(0, n, drain, 0)


def per_device(n, s_count, act, gain, wq, wk, wv, wo, cache, post):
    R, D = act.shape
    row_chunks = min(4, R // 16)
    s = lax.axis_index("seq")
    positions = (s * TOK_DEV + jnp.arange(TOK_DEV, dtype=jnp.int32)).astype(jnp.float32)
    cosine, sine = rope_tables(positions)
    bf, f32 = jnp.bfloat16, jnp.float32
    vmem = pl.BlockSpec(memory_space=pltpu.VMEM)
    hbm = pl.BlockSpec(memory_space=pl.ANY)
    dma = pltpu.SemaphoreType.DMA
    return pl.pallas_call(
        functools.partial(kernel, n, s_count),
        out_shape=jax.ShapeDtypeStruct((R, D), bf),
        in_specs=[vmem, vmem, hbm, hbm, hbm, hbm, hbm, vmem, vmem, vmem],
        out_specs=vmem,
        scratch_shapes=[
            pltpu.VMEM(wq.shape, bf),
            pltpu.VMEM(wk.shape, bf),
            pltpu.VMEM(wv.shape, bf),
            pltpu.VMEM(wo.shape, bf),
            pltpu.VMEM((n, R, D), bf),
            pltpu.VMEM((TOK_DEV, wq.shape[1]), bf),
            pltpu.VMEM((WINDOW + TOK_DEV, 2 * wk.shape[1]), bf),
            pltpu.VMEM((R, wo.shape[0]), bf),
            pltpu.VMEM((n + 1, COL_CHUNKS, R, D // COL_CHUNKS), bf),
            pltpu.VMEM((R, D), f32),
            dma((4,)),
            dma((REACH, 2)),
            dma((2, n, row_chunks)),
            dma((2, n, row_chunks)),
            dma((REACH, n)),
            dma((REACH, n)),
            dma((2, n, COL_CHUNKS)),
            dma((2, n, COL_CHUNKS)),
        ],
        compiler_params=pltpu.CompilerParams(
            collective_id=0, has_side_effects=True, vmem_limit_bytes=62 * 1024 * 1024
        ),
    )(act, gain, wq, wk, wv, wo, cache, post, cosine, sine)


def solution(mesh):
    return jax.shard_map(
        functools.partial(per_device, mesh.shape["head"], mesh.shape["seq"]),
        mesh=mesh,
        in_specs=(
            P(("seq", "head"), None),
            P(),
            P(None, "head"),
            P(None, "head"),
            P(None, "head"),
            P("head", None),
            P(None, None, "head"),
            P(),
        ),
        out_specs=P(("seq", "head"), None),
        check_vma=False,
    )
```
